32 devices in a mesh: tm: 8 (over z, core), space: 4 (over y, x).
Axes of the slice: x: 2, y: 2, z: 4, core: 2. Of those that a mesh axis runs over, the one named last changes fastest.
Arguments:
- features: bfloat16 [32, 64, 128, 128], P('tm', 'space'), may hold values from -6 to 6
- kernel_first: bfloat16 [3, 3, 3, 128, 128], replicated, may hold values from -0.109375 to 0.109375
- bias_first: float32 [128], replicated, may hold values from -3 to 3
- kernel_down: bfloat16 [3, 3, 128, 256], replicated, may hold values from -0.1875 to 0.1875
- bias_down: float32 [256], replicated, may hold values from -3 to 3
- kernel_second: bfloat16 [3, 3, 3, 256, 256], replicated, may hold values from -0.078125 to 0.078125
- bias_second: float32 [256], replicated, may hold values from -3 to 3
Outputs:
- latent: bfloat16 [32, 32, 64, 256], P('tm', 'space')
The draws below stay inside these ranges and needn't reach their ends.
All inputs are finite; a program needn't handle non-finite values.
Results may differ from the reference program's by a relative error of at most 0.0095.
Values may be sent and summed in bfloat16 or wider, within the bound.
A program may use at most 64 MiB of HBM per device.

```python
import jax
import jax.numpy as jnp
from jax import lax

C0 = 128
C1 = 256
COLS = 128
FRAMES = 32
ROWS = 64


def block_levels(stream_key, shape, shards, low, largest):
    def one(dim, shards_of):
        draws = jax.random.uniform(jax.random.fold_in(jax.random.fold_in(stream_key, 6), dim), (shards_of,), jnp.float32, low / len(shards), largest / len(shards))
        return jnp.repeat(jnp.exp(draws), shape[dim] // shards_of).reshape((-1,) + (1,) * (len(shape) - dim - 1))

    loudness = one(*shards[0])
    for cut in shards[1:]:
        loudness = loudness * one(*cut)
    return loudness


def scatter_about(own_key, shape, spread, most, split=(), held_as=jnp.bfloat16):
    drawn = spread * jax.random.normal(own_key, shape, jnp.float32)
    if split:
        drawn = drawn * block_levels(own_key, shape, split, -0.22, 0.18)
    return jnp.clip(drawn, -most, most).astype(held_as)


def setup_inputs(seed: int = 0) -> dict:
    arg_keys = jax.random.split(jax.random.key(seed), 8)
    features = scatter_about(arg_keys[0], (FRAMES, ROWS, COLS, C0), 1.0, 6.0, ((0, 8), (1, 4)))
    kernel_first = scatter_about(arg_keys[1], (3, 3, 3, C0, C0), (27 * C0) ** -0.5, 0.109375)
    bias_first = scatter_about(arg_keys[2], (C0,), 0.5, 3.0, (), jnp.float32)
    kernel_down = scatter_about(arg_keys[3], (3, 3, C0, C1), (9 * C0) ** -0.5, 0.1875)
    bias_down = scatter_about(arg_keys[4], (C1,), 0.5, 3.0, (), jnp.float32)
    kernel_second = scatter_about(arg_keys[5], (3, 3, 3, C1, C1), (27 * C1) ** -0.5, 0.078125)
    bias_second = scatter_about(arg_keys[6], (C1,), 0.5, 3.0, (), jnp.float32)
    return {"features": features, "kernel_first": kernel_first, "bias_first": bias_first, "kernel_down": kernel_down, "bias_down": bias_down, "kernel_second": kernel_second, "bias_second": bias_second}


def conv_causal(activated, weight):
    activated = lax.optimization_barrier(activated)
    inputs = activated.astype(jnp.float32)[None]
    result = lax.conv_general_dilated(inputs, weight.astype(jnp.float32), (1, 1, 1), ((2, 0), (1, 1), (1, 1)), dimension_numbers=("NDHWC", "DHWIO", "NDHWC"), precision=lax.Precision.HIGHEST)
    return result[0]


def reference(features, kernel_first, bias_first, kernel_down, bias_down, kernel_second, bias_second):
    act_in = jax.nn.silu(features.astype(jnp.float32)).astype(jnp.bfloat16)
    first_out = (features.astype(jnp.float32) + bias_first + conv_causal(act_in, kernel_first)).astype(jnp.bfloat16)
    first_out = lax.optimization_barrier(first_out)
    reduced = lax.conv_general_dilated(first_out.astype(jnp.float32), kernel_down.astype(jnp.float32), (2, 2), ((1, 1), (1, 1)), dimension_numbers=("NHWC", "HWIO", "NHWC"), precision=lax.Precision.HIGHEST)
    reduced = (reduced + bias_down).astype(jnp.bfloat16)
    reduced = lax.optimization_barrier(reduced)
    act_mid = jax.nn.silu(reduced.astype(jnp.float32)).astype(jnp.bfloat16)
    latent = (reduced.astype(jnp.float32) + bias_second + conv_causal(act_mid, kernel_second)).astype(jnp.bfloat16)
    return latent
```

```python
import functools

import jax
import jax.numpy as jnp
from jax import lax
from jax.experimental import pallas as pl
from jax.experimental.pallas import tpu as pltpu
from jax.sharding import PartitionSpec as P

MESH = pl.DeviceIdType.MESH
BF = jnp.bfloat16
F32 = jnp.float32


def silu(v):
    h = 0.5 * v
    return h + h * jnp.tanh(h)


def before(x, width):
    p = lax.broadcasted_iota(jnp.int32, x.shape, 0) % width
    return jnp.where(p == 0, 0.0, pltpu.roll(x, 1, 0))


def after(x, width):
    p = lax.broadcasted_iota(jnp.int32, x.shape, 0) % width
    return jnp.where(p == width - 1, 0.0, pltpu.roll(x, x.shape[0] - 1, 0))


def kernel(
    nt, ns, x, b1, bd, b2, k1, kd, k2, out,
    hx, hr, lines, act, feat, w1, wd, w2, fo, red, mid, res,
    send, recv, wsem, osem,
):
    t, s = lax.axis_index("tm"), lax.axis_index("space")
    frames, rows, cols, c0 = x.shape
    pairs = cols // 2
    half = rows // 2
    c1 = res.shape[-1]

    def there(dt, ds):
        ok = None
        for pos, step, count in ((t, dt, nt), (s, ds, ns)):
            if step:
                this = pos < count - 1 if step > 0 else pos > 0
                ok = this if ok is None else jnp.logical_and(ok, this)
        return ok

    around = [(dt, ds) for dt in (-1, 0, 1) for ds in (-1, 0, 1) if dt or ds]

    def place(dt, ds):
        return (lax.rem(t + dt + nt, nt), lax.rem(s + ds + ns, ns))

    weights = [
        pltpu.make_async_copy(src, dst, wsem.at[n])
        for n, (src, dst) in enumerate(
            [
                (k1.at[:, :, 1], w1.at[:, :, 0:c0, 0:c0]),
                (k1.at[:, :, 0], w1.at[:, :, 0:c0, c0:2 * c0]),
                (k1.at[:, :, 2], w1.at[:, :, 0:c0, 3 * c0:4 * c0]),
                (k1.at[:, :, 2], w1.at[:, :, c0:2 * c0, 0:c0]),
                (k1.at[:, :, 1], w1.at[:, :, c0:2 * c0, c0:2 * c0]),
                (k1.at[:, :, 0], w1.at[:, :, c0:2 * c0, 2 * c0:3 * c0]),
                (kd.at[:, 1], wd.at[:, 0:c0, 0:c1]),
                (kd.at[:, 2], wd.at[:, c0:2 * c0, 0:c1]),
                (kd.at[:, 0], wd.at[:, c0:2 * c0, c1:2 * c1]),
                (k2.at[:, :, 0], w2.at[:, :, :, 0:c1]),
                (k2.at[:, :, 1], w2.at[:, :, :, c1:2 * c1]),
                (k2.at[:, :, 2], w2.at[:, :, :, 2 * c1:3 * c1]),
            ]
        )
    ]
    for copy in weights:
        copy.start()

    barrier = pltpu.get_barrier_semaphore()
    for dt, ds in around:
        @pl.when(there(dt, ds))
        def _():
            pl.semaphore_signal(barrier, inc=1, device_id=place(dt, ds), device_id_type=MESH)
    near_t = jnp.where(t > 0, 1, 0) + jnp.where(t < nt - 1, 1, 0) + 1
    near_s = jnp.where(s > 0, 1, 0) + jnp.where(s < ns - 1, 1, 0) + 1
    pl.semaphore_wait(barrier, near_t * near_s - 1)

    plan = {}

    def add(name, src, dst, dt, ds):
        plan[name] = (src, dst, len(plan), dt, ds)

    last, prev = frames - 1, frames - 2
    add("up", x.at[:, 0], hr.at[1], 0, -1)
    add("down", x.at[:, rows - 1], hr.at[0], 0, 1)
    add("t1", x.at[last], hx.at[1, 1:rows + 1], 1, 0)
    add("tu", x.at[prev:frames, 0], hx.at[:, rows + 1], 1, -1)
    add("td", x.at[prev:frames, rows - 1], hx.at[:, 0], 1, 1)
    add("t0", x.at[prev], hx.at[0, 1:rows + 1], 1, 0)
    for f in range(frames):
        add(f"fo{f}", fo.at[f, rows], fo.at[f, 0], 0, 1)
        add(f"mu{f}", mid.at[f + 2, 1], mid.at[f + 2, half + 1], 0, -1)
        add(f"md{f}", mid.at[f + 2, half], mid.at[f + 2, 0], 0, 1)
        if f >= prev:
            g = f - prev
            add(f"mt{f}", mid.at[f + 2, 1:half + 1], mid.at[g, 1:half + 1], 1, 0)
            add(f"ma{f}", mid.at[f + 2, 1], mid.at[g, half + 1], 1, -1)
            add(f"mb{f}", mid.at[f + 2, half], mid.at[g, 0], 1, 1)

    def remote(name):
        src, dst, n, dt, ds = plan[name]
        return pltpu.make_async_remote_copy(
            src_ref=src, dst_ref=dst, send_sem=send.at[n], recv_sem=recv.at[n],
            device_id=place(dt, ds), device_id_type=MESH,
        )

    def start(*names):
        for name in names:
            @pl.when(there(*plan[name][3:]))
            def _():
                remote(name).start()

    def arrived(*names):
        for name in names:
            _, _, _, dt, ds = plan[name]
            @pl.when(there(-dt, -ds))
            def _():
                remote(name).wait_recv()

    start("up", "down", "t1", "tu", "td", "t0")

    @pl.when(t == 0)
    def _():
        hx[...] = jnp.zeros_like(hx)
        mid[0:2] = jnp.zeros((2,) + mid.shape[1:], BF)

    @pl.when(s == 0)
    def _():
        hr[0] = jnp.zeros(hr.shape[1:], BF)
        fo[:, 0] = jnp.zeros((frames, pairs, 2 * c0), BF)
        mid[2:, 0] = jnp.zeros((frames, pairs, c1), BF)

    @pl.when(s == ns - 1)
    def _():
        hr[1] = jnp.zeros(hr.shape[1:], BF)
        mid[2:, half + 1] = jnp.zeros((frames, pairs, c1), BF)

    @pl.when(jnp.logical_and(t > 0, s == 0))
    def _():
        hx[:, 0] = jnp.zeros((2, cols, c0), BF)
        mid[0:2, 0] = jnp.zeros((2, pairs, c1), BF)

    @pl.when(jnp.logical_and(t > 0, s == ns - 1))
    def _():
        hx[:, rows + 1] = jnp.zeros((2, cols, c0), BF)
        mid[0:2, half + 1] = jnp.zeros((2, pairs, c1), BF)

    w1[:, :, 0:c0, 2 * c0:3 * c0] = jnp.zeros((3, 3, c0, c0), BF)
    w1[:, :, c0:2 * c0, 3 * c0:4 * c0] = jnp.zeros((3, 3, c0, c0), BF)
    wd[:, 0:c0, c1:2 * c1] = jnp.zeros((3, c0, c1), BF)

    def paired(value):
        count = value.shape[0]
        lines[0:count * cols] = value.reshape(count * cols, c0).astype(F32)
        even = lines[pl.ds(0, count * pairs, stride=2), :]
        odd = lines[pl.ds(1, count * pairs, stride=2), :]
        both = jnp.concatenate([even, odd], axis=1)
        return both.reshape(count, pairs, 2 * c0)

    step = 4

    def own(n, carry):
        f, r = n // (rows // step), (n % (rows // step)) * step
        both = paired(x[f, pl.ds(r, step)])
        feat[f, pl.ds(r, step)] = both.astype(BF)
        act[f + 2, pl.ds(r + 1, step)] = silu(both).astype(BF)
        return carry

    lax.fori_loop(0, frames * rows // step, own, 0)
    arrived("up", "down")
    for side, row in ((0, 0), (1, rows + 1)):
        act[2:, row] = silu(paired(hr[side])).astype(BF)

    for copy in weights[:6]:
        copy.wait()

    block = 8

    def conv_first(f):
        def body(n, carry):
            r = n * block
            left = jnp.concatenate(
                [
                    act[f + i, pl.ds(r + j, block)].reshape(block * pairs, 2 * c0)
                    for i in range(3) for j in range(3)
                ],
                axis=1,
            )
            total = jnp.dot(left, w1[...].reshape(9 * 2 * c0, 4 * c0), preferred_element_type=F32)
            bias = b1[...]
            base = feat[f, pl.ds(r, block)].reshape(block * pairs, 2 * c0).astype(F32)
            even = base[:, :c0] + bias + total[:, :c0] + before(total[:, 2 * c0:3 * c0], pairs)
            odd = base[:, c0:] + bias + total[:, c0:2 * c0] + after(total[:, 3 * c0:], pairs)
            both = jnp.concatenate([even, odd], axis=1).astype(BF)
            fo[f, pl.ds(r + 1, block)] = both.reshape(block, pairs, 2 * c0)
            return carry

        lax.fori_loop(0, rows // block, body, 0)
        start(f"fo{f}")

    def downsample(f):
        arrived(f"fo{f}")
        left = jnp.concatenate(
            [
                jnp.concatenate([fo[f, 2 * r + j][None] for r in range(half)], axis=0).reshape(half * pairs, 2 * c0)
                for j in range(3)
            ],
            axis=1,
        )
        total = jnp.dot(left, wd[...].reshape(3 * 2 * c0, 2 * c1), preferred_element_type=F32)
        value = (total[:, :c1] + before(total[:, c1:], pairs) + bd[...]).astype(BF)
        red[f] = value.reshape(half, pairs, c1)
        mid[f + 2, 1:half + 1] = silu(value.astype(F32)).astype(BF).reshape(half, pairs, c1)
        if f >= prev:
            start(f"mt{f}", f"ma{f}", f"mb{f}")
        start(f"mu{f}", f"md{f}")

    def conv_second(f):
        left = jnp.concatenate(
            [
                mid[f + i, j:j + half].reshape(half * pairs, c1)
                for i in range(3) for j in range(3)
            ],
            axis=1,
        )
        total = jnp.dot(left, w2[...].reshape(9 * c1, 3 * c1), preferred_element_type=F32)
        value = red[f].reshape(half * pairs, c1).astype(F32) + b2[...]
        value = value + total[:, c1:2 * c1] + before(total[:, :c1], pairs) + after(total[:, 2 * c1:], pairs)
        res[f] = value.astype(BF).reshape(half, pairs, c1)
        pltpu.make_async_copy(res.at[f], out.at[f], osem.at[f]).start()

    def halo(g):
        def body(n, carry):
            act[g, pl.ds(n * 3, 3)] = silu(paired(hx[g, pl.ds(n * 3, 3)])).astype(BF)
            return carry

        lax.fori_loop(0, (rows + 2) // 3, body, 0)

    conv_first(3)
    conv_first(2)
    for copy in weights[6:9]:
        copy.wait()
    downsample(3)
    arrived("t1", "tu", "td")
    halo(1)
    conv_first(1)
    downsample(2)
    arrived("t0")
    halo(0)
    conv_first(0)
    downsample(1)
    downsample(0)
    for copy in weights[9:]:
        copy.wait()
    for f in range(frames):
        arrived(f"mu{f}", f"md{f}")
    conv_second(3)
    conv_second(2)
    arrived("mt3", "ma3", "mb3")
    conv_second(1)
    arrived("mt2", "ma2", "mb2")
    conv_second(0)

    for name in plan:
        @pl.when(there(*plan[name][3:]))
        def _():
            remote(name).wait_send()
    for f in range(frames):
        pltpu.make_async_copy(res.at[f], out.at[f], osem.at[f]).wait()


def on_device(nt, ns, x, k1, b1, kd, bd, k2, b2):
    frames, rows, cols, c0 = x.shape
    c1 = kd.shape[-1]
    half, pairs = rows // 2, cols // 2
    vmem = pl.BlockSpec(memory_space=pltpu.VMEM)
    hbm = pl.BlockSpec(memory_space=pl.ANY)
    copies = 6 + 3 * frames + 6
    return pl.pallas_call(
        functools.partial(kernel, nt, ns),
        out_shape=jax.ShapeDtypeStruct((frames, half, pairs, c1), BF),
        in_specs=[vmem] * 4 + [hbm] * 3,
        out_specs=hbm,
        scratch_shapes=[
            pltpu.VMEM((2, rows + 2, cols, c0), BF),
            pltpu.VMEM((2, frames, cols, c0), BF),
            pltpu.VMEM((4 * cols, c0), F32),
            pltpu.VMEM((frames + 2, rows + 2, pairs, 2 * c0), BF),
            pltpu.VMEM((frames, rows, pairs, 2 * c0), BF),
            pltpu.VMEM((3, 3, 2 * c0, 4 * c0), BF),
            pltpu.VMEM((3, 2 * c0, 2 * c1), BF),
            pltpu.VMEM((3, 3, c1, 3 * c1), BF),
            pltpu.VMEM((frames, rows + 1, pairs, 2 * c0), BF),
            pltpu.VMEM((frames, half, pairs, c1), BF),
            pltpu.VMEM((frames + 2, half + 2, pairs, c1), BF),
            pltpu.VMEM((frames, half, pairs, c1), BF),
            pltpu.SemaphoreType.DMA((copies,)),
            pltpu.SemaphoreType.DMA((copies,)),
            pltpu.SemaphoreType.DMA((12,)),
            pltpu.SemaphoreType.DMA((frames,)),
        ],
        compiler_params=pltpu.CompilerParams(
            collective_id=0, has_side_effects=True, vmem_limit_bytes=60 * 1024 * 1024
        ),
        cost_estimate=pl.CostEstimate(flops=16 * 10**9, bytes_accessed=10**7, transcendentals=0),
    )(x, b1[None], bd[None], b2[None], k1, kd, k2)


def solution(mesh):
    in_specs = (P("tm", "space", None, None), P(), P(), P(), P(), P(), P())
    out_specs = P("tm", "space", None, None)
    sizes = mesh.shape["tm"], mesh.shape["space"]
    return jax.shard_map(
        functools.partial(on_device, *sizes), mesh=mesh, in_specs=in_specs, out_specs=out_specs, check_vma=False
    )
```

```python
import functools

import jax
import jax.numpy as jnp
from jax import lax
from jax.experimental import pallas as pl
from jax.experimental.pallas import tpu as pltpu
from jax.sharding import PartitionSpec as P

MESH = pl.DeviceIdType.MESH
BF = jnp.bfloat16
F32 = jnp.float32


def silu(v):
    h = 0.5 * v
    return h + h * jnp.tanh(h)


def edge(shape, width, row):
    at = lax.broadcasted_iota(jnp.int32, (width, shape[1]), 0) == row
    return jnp.broadcast_to(at[None], (shape[0] // width,) + at.shape).reshape(shape)


def before(x, width):
    return jnp.where(edge(x.shape, width, 0), 0.0, pltpu.roll(x, 1, 0))


def after(x, width):
    return jnp.where(edge(x.shape, width, width - 1), 0.0, pltpu.roll(x, x.shape[0] - 1, 0))


def products(d0, d1, d2, d3):
    return d0 - d2, d1 + d2, d2 - d1, d1 - d3


def kernel(
    nt, ns, x, b1, bd, b2, k1, kd, k2, out,
    hx, hr, lines, act, feat, v1, u1, wd, v2, u2, fo, red, mid, res, sums,
    send, recv, wsem, osem,
):
    t, s = lax.axis_index("tm"), lax.axis_index("space")
    frames, rows, cols, c0 = x.shape
    pairs = cols // 2
    half = rows // 2
    c1 = res.shape[-1]

    def there(dt, ds):
        ok = None
        for pos, step, count in ((t, dt, nt), (s, ds, ns)):
            if step:
                this = pos < count - 1 if step > 0 else pos > 0
                ok = this if ok is None else jnp.logical_and(ok, this)
        return ok

    around = [(dt, ds) for dt in (-1, 0, 1) for ds in (-1, 0, 1) if dt or ds]

    def place(dt, ds):
        return (lax.rem(t + dt + nt, nt), lax.rem(s + ds + ns, ns))

    moves = []
    for j, slot in ((0, 0), (1, 1), (2, 3)):
        for k, blocks in ((0, ((0, 1), (1, 2))), (1, ((0, 0), (1, 1))), (2, ((0, 3), (1, 0)))):
            for a, b in blocks:
                moves.append((k1.at[:, j, k], u1.at[slot, :, a * c0:(a + 1) * c0, b * c0:(b + 1) * c0]))
    n_first = len(moves)
    moves.append((kd.at[:, 1], wd.at[:, 0:c0, 0:c1]))
    moves.append((kd.at[:, 2], wd.at[:, c0:2 * c0, 0:c1]))
    moves.append((kd.at[:, 0], wd.at[:, c0:2 * c0, c1:2 * c1]))
    n_down = len(moves)
    for j, slot in ((0, 0), (1, 1), (2, 3)):
        for k in range(3):
            moves.append((k2.at[:, j, k], u2.at[slot, :, :, k * c1:(k + 1) * c1]))
    weights = [pltpu.make_async_copy(src, dst, wsem.at[n]) for n, (src, dst) in enumerate(moves)]
    for copy in weights:
        copy.start()

    barrier = pltpu.get_barrier_semaphore()
    for dt, ds in around:
        @pl.when(there(dt, ds))
        def _():
            pl.semaphore_signal(barrier, inc=1, device_id=place(dt, ds), device_id_type=MESH)
    near_t = jnp.where(t > 0, 1, 0) + jnp.where(t < nt - 1, 1, 0) + 1
    near_s = jnp.where(s > 0, 1, 0) + jnp.where(s < ns - 1, 1, 0) + 1
    pl.semaphore_wait(barrier, near_t * near_s - 1)

    plan = {}

    def add(name, src, dst, dt, ds):
        plan[name] = (src, dst, len(plan), dt, ds)

    last, prev = frames - 1, frames - 2
    add("up", x.at[:, 0], hr.at[1], 0, -1)
    add("down", x.at[:, rows - 1], hr.at[0], 0, 1)
    add("t1", x.at[last], hx.at[1, 1:rows + 1], 1, 0)
    add("tu", x.at[prev:frames, 0], hx.at[:, rows + 1], 1, -1)
    add("td", x.at[prev:frames, rows - 1], hx.at[:, 0], 1, 1)
    add("t0", x.at[prev], hx.at[0, 1:rows + 1], 1, 0)
    for f in range(frames):
        add(f"fo{f}", fo.at[f, rows], fo.at[f, 0], 0, 1)
        add(f"mu{f}", mid.at[f + 2, 1], mid.at[f + 2, half + 1], 0, -1)
        add(f"md{f}", mid.at[f + 2, half], mid.at[f + 2, 0], 0, 1)
        if f >= prev:
            g = f - prev
            add(f"mt{f}", mid.at[f + 2, 1:half + 1], mid.at[g, 1:half + 1], 1, 0)
            add(f"ma{f}", mid.at[f + 2, 1], mid.at[g, half + 1], 1, -1)
            add(f"mb{f}", mid.at[f + 2, half], mid.at[g, 0], 1, 1)

    def remote(name):
        src, dst, n, dt, ds = plan[name]
        return pltpu.make_async_remote_copy(
            src_ref=src, dst_ref=dst, send_sem=send.at[n], recv_sem=recv.at[n],
            device_id=place(dt, ds), device_id_type=MESH,
        )

    def start(*names):
        for name in names:
            @pl.when(there(*plan[name][3:]))
            def _():
                remote(name).start()

    def arrived(*names):
        for name in names:
            _, _, _, dt, ds = plan[name]
            @pl.when(there(-dt, -ds))
            def _():
                remote(name).wait_recv()

    start("up", "down", "t1", "tu", "td", "t0")

    @pl.when(t == 0)
    def _():
        hx[...] = jnp.zeros_like(hx)
        mid[0:2] = jnp.zeros((2,) + mid.shape[1:], BF)

    @pl.when(s == 0)
    def _():
        hr[0] = jnp.zeros(hr.shape[1:], BF)
        fo[:, 0] = jnp.zeros((frames, pairs, 2 * c0), BF)
        mid[2:, 0] = jnp.zeros((frames, pairs, c1), BF)

    @pl.when(s == ns - 1)
    def _():
        hr[1] = jnp.zeros(hr.shape[1:], BF)
        mid[2:, half + 1] = jnp.zeros((frames, pairs, c1), BF)

    @pl.when(jnp.logical_and(t > 0, s == 0))
    def _():
        hx[:, 0] = jnp.zeros((2, cols, c0), BF)
        mid[0:2, 0] = jnp.zeros((2, pairs, c1), BF)

    @pl.when(jnp.logical_and(t > 0, s == ns - 1))
    def _():
        hx[:, rows + 1] = jnp.zeros((2, cols, c0), BF)
        mid[0:2, half + 1] = jnp.zeros((2, pairs, c1), BF)

    for slot in (0, 1, 3):
        u1[slot, :, 0:c0, 2 * c0:3 * c0] = jnp.zeros((3, c0, c0), BF)
        u1[slot, :, c0:2 * c0, 3 * c0:4 * c0] = jnp.zeros((3, c0, c0), BF)
    wd[:, 0:c0, c1:2 * c1] = jnp.zeros((3, c0, c1), BF)

    def paired(value):
        count = value.shape[0]
        lines[0:count * cols] = value.reshape(count * cols, c0).astype(F32)
        even = lines[pl.ds(0, count * pairs, stride=2), :]
        odd = lines[pl.ds(1, count * pairs, stride=2), :]
        both = jnp.concatenate([even, odd], axis=1)
        return both.reshape(count, pairs, 2 * c0)

    step = 4

    def own(n, carry):
        f, r = n // (rows // step), (n % (rows // step)) * step
        both = paired(x[f, pl.ds(r, step)])
        feat[f, pl.ds(r, step)] = both.astype(BF)
        act[f + 2, pl.ds(r + 1, step)] = silu(both).astype(BF)
        return carry

    lax.fori_loop(0, frames * rows // step, own, 0)
    arrived("up", "down")
    for side, row in ((0, 0), (1, rows + 1)):
        act[2:, row] = silu(paired(hr[side])).astype(BF)

    def taps(u):
        step = 32
        per = u.shape[2] // step

        def body(n, carry):
            i, r = n // per, pl.multiple_of((n % per) * step, step)
            g0, g1, g2 = (0.5 * u[m, i, pl.ds(r, step)].astype(F32) for m in (0, 1, 3))
            u[1, i, pl.ds(r, step)] = (g0 + g2 + g1).astype(BF)
            u[2, i, pl.ds(r, step)] = (g0 + g2 - g1).astype(BF)
            return carry

        lax.fori_loop(0, 3 * per, body, 0)

    def transform(src, dst, g):
        def body(n, carry):
            cells = products(*[src[g, 2 * n + j] for j in range(4)])
            for m in range(4):
                dst[g, m, n] = cells[m]
            return carry

        lax.fori_loop(0, dst.shape[2], body, 0)

    def filtered(v, u, group):
        width = v.shape[-1]
        size = v.shape[2] * pairs
        n_out = u.shape[-1]
        held = sums.at[:, :, 0:n_out]
        for m in range(4):
            left = jnp.concatenate(
                [
                    jnp.concatenate([v[f + i, m].reshape(size, width) for i in range(3)], axis=1)
                    for f in group
                ],
                axis=0,
            )
            right = u[m].reshape(3 * width, u.shape[-1])
            held[m] = jnp.dot(left, right, preferred_element_type=F32)
        return held[0] + held[1] + held[2], held[1] - held[2] - held[3]

    def conv_first(f):
        bias = b1[...]
        for parity, total in enumerate(filtered(v1, u1, [f])):
            base = jnp.concatenate([feat[f, 2 * n + parity] for n in range(half)], axis=0).astype(F32)
            even = base[:, :c0] + bias + total[:, :c0] + before(total[:, 2 * c0:3 * c0], pairs)
            odd = base[:, c0:] + bias + total[:, c0:2 * c0] + after(total[:, 3 * c0:], pairs)
            both = jnp.concatenate([even, odd], axis=1).astype(BF).reshape(half, pairs, 2 * c0)
            for n in range(half):
                fo[f, 2 * n + parity + 1] = both[n]
        start(f"fo{f}")

    def downsample(f):
        arrived(f"fo{f}")
        left = jnp.concatenate(
            [
                jnp.concatenate([fo[f, 2 * r + j][None] for r in range(half)], axis=0).reshape(half * pairs, 2 * c0)
                for j in range(3)
            ],
            axis=1,
        )
        total = jnp.dot(left, wd[...].reshape(3 * 2 * c0, 2 * c1), preferred_element_type=F32)
        value = (total[:, :c1] + before(total[:, c1:], pairs) + bd[...]).astype(BF)
        red[f] = value.reshape(half, pairs, c1)
        mid[f + 2, 1:half + 1] = silu(value.astype(F32)).astype(BF).reshape(half, pairs, c1)
        if f >= prev:
            start(f"mt{f}", f"ma{f}", f"mb{f}")
        start(f"mu{f}", f"md{f}")

    def conv_second(group):
        quarter = half // 2
        for parity, total in enumerate(filtered(v2, u2, group)):
            base = jnp.concatenate(
                [red[f, 2 * n + parity] for f in group for n in range(quarter)], axis=0
            ).astype(F32)
            value = base + b2[...] + total[:, c1:2 * c1]
            value = value + before(total[:, :c1], pairs) + after(total[:, 2 * c1:], pairs)
            value = value.astype(BF).reshape(len(group) * quarter, pairs, c1)
            for g, f in enumerate(group):
                for n in range(quarter):
                    res[f, 2 * n + parity] = value[g * quarter + n]
        for f in group:
            pltpu.make_async_copy(res.at[f], out.at[f], osem.at[f]).start()

    def halo(g):
        def body(n, carry):
            act[g, pl.ds(n * 3, 3)] = silu(paired(hx[g, pl.ds(n * 3, 3)])).astype(BF)
            return carry

        lax.fori_loop(0, (rows + 2) // 3, body, 0)
        transform(act, v1, g)

    for copy in weights[:n_first]:
        copy.wait()
    taps(u1)
    for g in range(2, frames + 2):
        transform(act, v1, g)

    conv_first(last)
    conv_first(prev)
    for copy in weights[n_first:n_down]:
        copy.wait()
    downsample(last)
    for copy in weights[n_down:]:
        copy.wait()
    taps(u2)
    arrived("t1", "tu", "td")
    halo(1)
    conv_first(1)
    downsample(prev)
    arrived("t0")
    halo(0)
    conv_first(0)
    downsample(1)
    downsample(0)
    for f in reversed(range(frames)):
        arrived(f"mu{f}", f"md{f}")
        transform(mid, v2, f + 2)
    conv_second([last, prev])
    for f in (last, prev):
        arrived(f"mt{f}", f"ma{f}", f"mb{f}")
        transform(mid, v2, f - prev)
    conv_second([1, 0])

    for name in plan:
        @pl.when(there(*plan[name][3:]))
        def _():
            remote(name).wait_send()
    for f in range(frames):
        pltpu.make_async_copy(res.at[f], out.at[f], osem.at[f]).wait()


def on_device(nt, ns, x, k1, b1, kd, bd, k2, b2):
    frames, rows, cols, c0 = x.shape
    c1 = kd.shape[-1]
    half, pairs = rows // 2, cols // 2
    vmem = pl.BlockSpec(memory_space=pltpu.VMEM)
    hbm = pl.BlockSpec(memory_space=pl.ANY)
    copies = 6 + 3 * frames + 6
    return pl.pallas_call(
        functools.partial(kernel, nt, ns),
        out_shape=jax.ShapeDtypeStruct((frames, half, pairs, c1), BF),
        in_specs=[vmem] * 4 + [hbm] * 3,
        out_specs=hbm,
        scratch_shapes=[
            pltpu.VMEM((2, rows + 2, cols, c0), BF),
            pltpu.VMEM((2, frames, cols, c0), BF),
            pltpu.VMEM((4 * cols, c0), F32),
            pltpu.VMEM((frames + 2, rows + 2, pairs, 2 * c0), BF),
            pltpu.VMEM((frames, rows, pairs, 2 * c0), BF),
            pltpu.VMEM((frames + 2, 4, half, pairs, 2 * c0), BF),
            pltpu.VMEM((4, 3, 2 * c0, 4 * c0), BF),
            pltpu.VMEM((3, 2 * c0, 2 * c1), BF),
            pltpu.VMEM((frames + 2, 4, half // 2, pairs, c1), BF),
            pltpu.VMEM((4, 3, c1, 3 * c1), BF),
            pltpu.VMEM((frames, rows + 1, pairs, 2 * c0), BF),
            pltpu.VMEM((frames, half, pairs, c1), BF),
            pltpu.VMEM((frames + 2, half + 2, pairs, c1), BF),
            pltpu.VMEM((frames, half, pairs, c1), BF),
            pltpu.VMEM((4, half * pairs, 3 * c1), F32),
            pltpu.SemaphoreType.DMA((copies,)),
            pltpu.SemaphoreType.DMA((copies,)),
            pltpu.SemaphoreType.DMA((30,)),
            pltpu.SemaphoreType.DMA((frames,)),
        ],
        compiler_params=pltpu.CompilerParams(
            collective_id=0, has_side_effects=True, vmem_limit_bytes=60 * 1024 * 1024
        ),
        cost_estimate=pl.CostEstimate(flops=16 * 10**9, bytes_accessed=10**7, transcendentals=0),
    )(x, b1[None], bd[None], b2[None], k1, kd, k2)


def solution(mesh):
    in_specs = (P("tm", "space", None, None), P(), P(), P(), P(), P(), P())
    out_specs = P("tm", "space", None, None)
    sizes = mesh.shape["tm"], mesh.shape["space"]
    return jax.shard_map(
        functools.partial(on_device, *sizes), mesh=mesh, in_specs=in_specs, out_specs=out_specs, check_vma=False
    )
```

```python
import functools

import jax
import jax.numpy as jnp
from jax import lax
from jax.experimental import pallas as pl
from jax.experimental.pallas import tpu as pltpu
from jax.sharding import PartitionSpec as P

MESH = pl.DeviceIdType.MESH
BF = jnp.bfloat16
F32 = jnp.float32


def silu(v):
    h = 0.5 * v
    return h + h * jnp.tanh(h)


def edge(shape, width, row):
    at = lax.broadcasted_iota(jnp.int32, (width, shape[1]), 0) == row
    return jnp.broadcast_to(at[None], (shape[0] // width,) + at.shape).reshape(shape)


def before(x, width):
    return jnp.where(edge(x.shape, width, 0), 0.0, pltpu.roll(x, 1, 0))


def after(x, width):
    return jnp.where(edge(x.shape, width, width - 1), 0.0, pltpu.roll(x, x.shape[0] - 1, 0))


def products(d0, d1, d2, d3):
    return d0 - d2, d1 + d2, d2 - d1, d1 - d3


def kernel(
    nt, ns, x, b1, bd, b2, k1, kd, k2, out,
    raw, lines, act, feat, v1, u1, wd, v2, u2, fo, red, mid, res, sums,
    send, recv, wsem, osem, xsem,
):
    t, s = lax.axis_index("tm"), lax.axis_index("space")
    frames, rows, cols, c0 = x.shape
    pairs = cols // 2
    half = rows // 2
    c1 = res.shape[-1]

    def there(dt, ds):
        ok = None
        for pos, step, count in ((t, dt, nt), (s, ds, ns)):
            if step:
                this = pos < count - 1 if step > 0 else pos > 0
                ok = this if ok is None else jnp.logical_and(ok, this)
        return ok

    around = [(dt, ds) for dt in (-1, 0, 1) for ds in (-1, 0, 1) if dt or ds]

    def place(dt, ds):
        return (lax.rem(t + dt + nt, nt), lax.rem(s + ds + ns, ns))

    moves = []
    for j, slot in ((0, 0), (1, 1), (2, 3)):
        for k, blocks in ((0, ((0, 1), (1, 2))), (1, ((0, 0), (1, 1))), (2, ((0, 3), (1, 0)))):
            for a, b in blocks:
                moves.append((k1.at[:, j, k], u1.at[slot, :, a * c0:(a + 1) * c0, b * c0:(b + 1) * c0]))
    n_first = len(moves)
    moves.append((kd.at[:, 1], wd.at[:, 0:c0, 0:c1]))
    moves.append((kd.at[:, 2], wd.at[:, c0:2 * c0, 0:c1]))
    moves.append((kd.at[:, 0], wd.at[:, c0:2 * c0, c1:2 * c1]))
    n_down = len(moves)
    for j, slot in ((0, 0), (1, 1), (2, 3)):
        for k in range(3):
            moves.append((k2.at[:, j, k], u2.at[slot, :, :, k * c1:(k + 1) * c1]))
    loads = [pltpu.make_async_copy(x.at[f], raw.at[f], xsem.at[f]) for f in range(frames)]
    for copy in reversed(loads):
        copy.start()
    weights = [pltpu.make_async_copy(src, dst, wsem.at[n]) for n, (src, dst) in enumerate(moves)]
    for copy in weights:
        copy.start()

    barrier = pltpu.get_barrier_semaphore()
    for dt, ds in around:
        @pl.when(there(dt, ds))
        def _():
            pl.semaphore_signal(barrier, inc=1, device_id=place(dt, ds), device_id_type=MESH)
    near_t = jnp.where(t > 0, 1, 0) + jnp.where(t < nt - 1, 1, 0) + 1
    near_s = jnp.where(s > 0, 1, 0) + jnp.where(s < ns - 1, 1, 0) + 1

    plan = {}

    def add(name, src, dst, dt, ds):
        plan[name] = (src, dst, len(plan), dt, ds)

    last, prev = frames - 1, frames - 2
    for f in range(frames):
        add(f"fo{f}", fo.at[f, rows], fo.at[f, 0], 0, 1)
        for kind, ref, end in (("a", act, rows), ("m", mid, half)):
            add(f"{kind}u{f}", ref.at[f + 2, 1], ref.at[f + 2, end + 1], 0, -1)
            add(f"{kind}d{f}", ref.at[f + 2, end], ref.at[f + 2, 0], 0, 1)
            if f >= prev:
                g = f - prev
                add(f"{kind}t{f}", ref.at[f + 2, 1:end + 1], ref.at[g, 1:end + 1], 1, 0)
                add(f"{kind}x{f}", ref.at[f + 2, 1], ref.at[g, end + 1], 1, -1)
                add(f"{kind}y{f}", ref.at[f + 2, end], ref.at[g, 0], 1, 1)

    def remote(name):
        src, dst, n, dt, ds = plan[name]
        return pltpu.make_async_remote_copy(
            src_ref=src, dst_ref=dst, send_sem=send.at[n], recv_sem=recv.at[n],
            device_id=place(dt, ds), device_id_type=MESH,
        )

    def start(*names):
        for name in names:
            @pl.when(there(*plan[name][3:]))
            def _():
                remote(name).start()

    def arrived(*names):
        for name in names:
            _, _, _, dt, ds = plan[name]
            @pl.when(there(-dt, -ds))
            def _():
                remote(name).wait_recv()

    def send_frame(kind, f):
        if f >= prev:
            start(f"{kind}t{f}", f"{kind}x{f}", f"{kind}y{f}")
        start(f"{kind}u{f}", f"{kind}d{f}")

    def borders(kind, f):
        arrived(f"{kind}u{f}", f"{kind}d{f}")

    def earlier(kind, f):
        arrived(f"{kind}t{f}", f"{kind}x{f}", f"{kind}y{f}")

    for ref, end in ((act, rows), (mid, half)):
        line = ref.shape[2:]

        @pl.when(t == 0)
        def _():
            ref[0:2] = jnp.zeros((2,) + ref.shape[1:], BF)

        for here, row in ((s == 0, 0), (s == ns - 1, end + 1)):
            @pl.when(here)
            def _():
                ref[2:, row] = jnp.zeros((frames,) + line, BF)

            @pl.when(jnp.logical_and(t > 0, here))
            def _():
                ref[0:2, row] = jnp.zeros((2,) + line, BF)

    @pl.when(s == 0)
    def _():
        fo[:, 0] = jnp.zeros((frames, pairs, 2 * c0), BF)

    for slot in (0, 1, 3):
        u1[slot, :, 0:c0, 2 * c0:3 * c0] = jnp.zeros((3, c0, c0), BF)
        u1[slot, :, c0:2 * c0, 3 * c0:4 * c0] = jnp.zeros((3, c0, c0), BF)
    wd[:, 0:c0, c1:2 * c1] = jnp.zeros((3, c0, c1), BF)

    step = 4

    def prepare(f, r, slot):
        count = step * cols
        base = slot * count
        lines[base:base + count] = raw[f, pl.ds(r, step)].reshape(count, c0).astype(F32)
        even = lines[pl.ds(base, count // 2, stride=2), :]
        odd = lines[pl.ds(base + 1, count // 2, stride=2), :]
        both = jnp.concatenate([even, odd], axis=1).reshape(step, pairs, 2 * c0)
        feat[f, pl.ds(r, step)] = both.astype(BF)
        act[f + 2, pl.ds(r + 1, step)] = silu(both).astype(BF)

    def own(f):
        def body(n, carry):
            for slot in range(2):
                prepare(f, (2 * n + slot) * step, slot)
            return carry

        lax.fori_loop(0, rows // (2 * step), body, 0)

    def taps(u, i):
        size = 32
        for r in range(0, u.shape[2], size):
            outer = u[0, i, r:r + size] + u[3, i, r:r + size]
            inner = u[1, i, r:r + size]
            u[1, i, r:r + size] = (outer + inner) * 0.5
            u[2, i, r:r + size] = (outer - inner) * 0.5

    def transform(src, dst, g):
        for n in range(dst.shape[2]):
            cells = products(*[src[g, 2 * n + j] for j in range(4)])
            for m in range(4):
                dst[g, m, n] = cells[m]

    def filtered(v, u, group, beside=None):
        width = v.shape[-1]
        size = v.shape[2] * pairs
        n_out = u.shape[-1]
        held = sums.at[:, 0:len(group) * size, 0:n_out]
        for m in range(4):
            left = jnp.concatenate(
                [
                    jnp.concatenate([v[f + i, m].reshape(size, width) for i in range(3)], axis=1)
                    for f in group
                ],
                axis=0,
            )
            right = u[m].reshape(3 * width, u.shape[-1])
            held[m] = jnp.dot(left, right, preferred_element_type=F32)
            if beside:
                beside(m)
        return held[0] + held[1] + held[2], held[1] - held[2] - held[3]

    def conv_first(f, beside=None):
        bias = b1[...]
        for parity, total in enumerate(filtered(v1, u1, [f], beside)):
            base = jnp.concatenate([feat[f, 2 * n + parity] for n in range(half)], axis=0).astype(F32)
            even = base[:, :c0] + bias + total[:, :c0] + before(total[:, 2 * c0:3 * c0], pairs)
            odd = base[:, c0:] + bias + total[:, c0:2 * c0] + after(total[:, 3 * c0:], pairs)
            both = jnp.concatenate([even, odd], axis=1).astype(BF).reshape(half, pairs, 2 * c0)
            for n in range(half):
                fo[f, 2 * n + parity + 1] = both[n]
        start(f"fo{f}")

    def downsample(f):
        arrived(f"fo{f}")
        left = jnp.concatenate(
            [
                jnp.concatenate([fo[f, 2 * r + j][None] for r in range(half)], axis=0).reshape(half * pairs, 2 * c0)
                for j in range(3)
            ],
            axis=1,
        )
        total = jnp.dot(left, wd[...].reshape(3 * 2 * c0, 2 * c1), preferred_element_type=F32)
        value = (total[:, :c1] + before(total[:, c1:], pairs) + bd[...]).astype(BF)
        red[f] = value.reshape(half, pairs, c1)
        mid[f + 2, 1:half + 1] = silu(value.astype(F32)).astype(BF).reshape(half, pairs, c1)
        send_frame("m", f)

    def conv_second(group):
        quarter = half // 2
        for parity, total in enumerate(filtered(v2, u2, group)):
            base = jnp.concatenate(
                [red[f, 2 * n + parity] for f in group for n in range(quarter)], axis=0
            ).astype(F32)
            value = base + b2[...] + total[:, c1:2 * c1]
            value = value + before(total[:, :c1], pairs) + after(total[:, 2 * c1:], pairs)
            value = value.astype(BF).reshape(len(group) * quarter, pairs, c1)
            for g, f in enumerate(group):
                for n in range(quarter):
                    res[f, 2 * n + parity] = value[g * quarter + n]
        for f in group:
            pltpu.make_async_copy(res.at[f], out.at[f], osem.at[f]).start()

    def prepare_first(m):
        for n in range(m, rows // step, 4):
            prepare(0, n * step, 0)

    def second_taps(m):
        if m < 3:
            taps(u2, m)

    for f in range(last, 0, -1):
        loads[f].wait()
        own(f)
        if f == last:
            pl.semaphore_wait(barrier, near_t * near_s - 1)
        send_frame("a", f)
    loads[0].wait()
    for copy in weights[:n_first]:
        copy.wait()
    for i in range(3):
        taps(u1, i)
    for f in range(last, 0, -1):
        borders("a", f)
        transform(act, v1, f + 2)
    conv_first(last, prepare_first)
    send_frame("a", 0)
    for copy in weights[n_first:]:
        copy.wait()
    borders("a", 0)
    transform(act, v1, 2)
    conv_first(prev, second_taps)
    downsample(last)
    earlier("a", last)
    transform(act, v1, 1)
    conv_first(1)
    downsample(prev)
    earlier("a", prev)
    transform(act, v1, 0)
    conv_first(0)
    downsample(1)
    for f in (last, prev):
        borders("m", f)
        transform(mid, v2, f + 2)
    downsample(0)
    borders("m", 1)
    transform(mid, v2, 3)
    conv_second([last])
    borders("m", 0)
    for f in (last, prev):
        earlier("m", f)
    for g in range(3):
        transform(mid, v2, g)
    conv_second(list(range(prev, -1, -1)))

    for name in plan:
        @pl.when(there(*plan[name][3:]))
        def _():
            remote(name).wait_send()
    for f in range(frames):
        pltpu.make_async_copy(res.at[f], out.at[f], osem.at[f]).wait()


def on_device(nt, ns, x, k1, b1, kd, bd, k2, b2):
    frames, rows, cols, c0 = x.shape
    c1 = kd.shape[-1]
    half, pairs = rows // 2, cols // 2
    vmem = pl.BlockSpec(memory_space=pltpu.VMEM)
    hbm = pl.BlockSpec(memory_space=pl.ANY)
    copies = 5 * frames + 12
    return pl.pallas_call(
        functools.partial(kernel, nt, ns),
        out_shape=jax.ShapeDtypeStruct((frames, half, pairs, c1), BF),
        in_specs=[hbm] + [vmem] * 3 + [hbm] * 3,
        out_specs=hbm,
        scratch_shapes=[
            pltpu.VMEM((frames, rows, cols, c0), BF),
            pltpu.VMEM((8 * cols, c0), F32),
            pltpu.VMEM((frames + 2, rows + 2, pairs, 2 * c0), BF),
            pltpu.VMEM((frames, rows, pairs, 2 * c0), BF),
            pltpu.VMEM((frames + 2, 4, half, pairs, 2 * c0), BF),
            pltpu.VMEM((4, 3, 2 * c0, 4 * c0), BF),
            pltpu.VMEM((3, 2 * c0, 2 * c1), BF),
            pltpu.VMEM((frames + 2, 4, half // 2, pairs, c1), BF),
            pltpu.VMEM((4, 3, c1, 3 * c1), BF),
            pltpu.VMEM((frames, rows + 1, pairs, 2 * c0), BF),
            pltpu.VMEM((frames, half, pairs, c1), BF),
            pltpu.VMEM((frames + 2, half + 2, pairs, c1), BF),
            pltpu.VMEM((frames, half, pairs, c1), BF),
            pltpu.VMEM((4, max(half, 3 * half // 2) * pairs, 3 * c1), F32),
            pltpu.SemaphoreType.DMA((copies,)),
            pltpu.SemaphoreType.DMA((copies,)),
            pltpu.SemaphoreType.DMA((30,)),
            pltpu.SemaphoreType.DMA((frames,)),
            pltpu.SemaphoreType.DMA((frames,)),
        ],
        compiler_params=pltpu.CompilerParams(
            collective_id=0, has_side_effects=True, vmem_limit_bytes=60 * 1024 * 1024
        ),
        cost_estimate=pl.CostEstimate(flops=16 * 10**9, bytes_accessed=10**7, transcendentals=0),
    )(x, b1[None], bd[None], b2[None], k1, kd, k2)


def solution(mesh):
    in_specs = (P("tm", "space", None, None), P(), P(), P(), P(), P(), P())
    out_specs = P("tm", "space", None, None)
    sizes = mesh.shape["tm"], mesh.shape["space"]
    return jax.shard_map(
        functools.partial(on_device, *sizes), mesh=mesh, in_specs=in_specs, out_specs=out_specs, check_vma=False
    )
```

```python
import functools

import jax
import jax.numpy as jnp
from jax import lax
from jax.experimental import pallas as pl
from jax.experimental.pallas import tpu as pltpu
from jax.sharding import PartitionSpec as P

MESH = pl.DeviceIdType.MESH
BF = jnp.bfloat16
F32 = jnp.float32


def silu(v):
    h = 0.5 * v
    return h + h * jnp.tanh(h)


def edge(shape, width, row):
    at = lax.broadcasted_iota(jnp.int32, (width, shape[1]), 0) == row
    return jnp.broadcast_to(at[None], (shape[0] // width,) + at.shape).reshape(shape)


def before(x, width):
    return jnp.where(edge(x.shape, width, 0), 0.0, pltpu.roll(x, 1, 0))


def after(x, width):
    return jnp.where(edge(x.shape, width, width - 1), 0.0, pltpu.roll(x, x.shape[0] - 1, 0))


def products(d0, d1, d2, d3):
    return d0 - d2, d1 + d2, d2 - d1, d1 - d3


def kernel(
    nt, ns, x, b1, bd, b2, k1, kd, k2, out,
    raw, lines, act, feat, v1, u1, wd, v2, u2, fo, red, mid, res, sums,
    send, recv, wsem, osem, xsem,
):
    t, s = lax.axis_index("tm"), lax.axis_index("space")
    frames, rows, cols, c0 = x.shape
    pairs = cols // 2
    half = rows // 2
    c1 = res.shape[-1]

    def there(dt, ds):
        ok = None
        for pos, step, count in ((t, dt, nt), (s, ds, ns)):
            if step:
                this = pos < count - 1 if step > 0 else pos > 0
                ok = this if ok is None else jnp.logical_and(ok, this)
        return ok

    around = [(dt, ds) for dt in (-1, 0, 1) for ds in (-1, 0, 1) if dt or ds]

    def place(dt, ds):
        return (lax.rem(t + dt + nt, nt), lax.rem(s + ds + ns, ns))

    moves = []
    for j, slot in ((0, 0), (1, 1), (2, 3)):
        for k, blocks in ((0, ((0, 1), (1, 2))), (1, ((0, 0), (1, 1))), (2, ((0, 3), (1, 0)))):
            for a, b in blocks:
                moves.append((k1.at[:, j, k], u1.at[slot, :, a * c0:(a + 1) * c0, b * c0:(b + 1) * c0]))
    n_first = len(moves)
    moves.append((kd.at[:, 1], wd.at[:, 0:c0, 0:c1]))
    moves.append((kd.at[:, 2], wd.at[:, c0:2 * c0, 0:c1]))
    moves.append((kd.at[:, 0], wd.at[:, c0:2 * c0, c1:2 * c1]))
    n_down = len(moves)
    for j, slot in ((0, 0), (1, 1), (2, 3)):
        for k in range(3):
            moves.append((k2.at[:, j, k], u2.at[slot, :, :, k * c1:(k + 1) * c1]))
    loads = [pltpu.make_async_copy(x.at[f], raw.at[f], xsem.at[f]) for f in range(frames)]
    for copy in reversed(loads):
        copy.start()
    weights = [pltpu.make_async_copy(src, dst, wsem.at[n]) for n, (src, dst) in enumerate(moves)]
    for copy in weights:
        copy.start()

    barrier = pltpu.get_barrier_semaphore()
    for dt, ds in around:
        @pl.when(there(dt, ds))
        def _():
            pl.semaphore_signal(barrier, inc=1, device_id=place(dt, ds), device_id_type=MESH)
    near_t = jnp.where(t > 0, 1, 0) + jnp.where(t < nt - 1, 1, 0) + 1
    near_s = jnp.where(s > 0, 1, 0) + jnp.where(s < ns - 1, 1, 0) + 1

    plan = {}

    def add(name, src, dst, dt, ds):
        plan[name] = (src, dst, len(plan), dt, ds)

    last, prev = frames - 1, frames - 2
    for f in range(frames):
        add(f"fo{f}", fo.at[f, rows], fo.at[f, 0], 0, 1)
        for kind, ref, end in (("a", act, rows), ("m", mid, half)):
            add(f"{kind}u{f}", ref.at[f + 2, 1], ref.at[f + 2, end + 1], 0, -1)
            add(f"{kind}d{f}", ref.at[f + 2, end], ref.at[f + 2, 0], 0, 1)
            if f >= prev:
                g = f - prev
                add(f"{kind}t{f}", ref.at[f + 2, 1:end + 1], ref.at[g, 1:end + 1], 1, 0)
                add(f"{kind}x{f}", ref.at[f + 2, 1], ref.at[g, end + 1], 1, -1)
                add(f"{kind}y{f}", ref.at[f + 2, end], ref.at[g, 0], 1, 1)

    def remote(name):
        src, dst, n, dt, ds = plan[name]
        return pltpu.make_async_remote_copy(
            src_ref=src, dst_ref=dst, send_sem=send.at[n], recv_sem=recv.at[n],
            device_id=place(dt, ds), device_id_type=MESH,
        )

    def start(*names):
        for name in names:
            @pl.when(there(*plan[name][3:]))
            def _():
                remote(name).start()

    def arrived(*names):
        for name in names:
            _, _, _, dt, ds = plan[name]
            @pl.when(there(-dt, -ds))
            def _():
                remote(name).wait_recv()

    def send_borders(kind, f):
        start(f"{kind}u{f}", f"{kind}d{f}")

    def send_later(kind, f):
        if f >= prev:
            start(f"{kind}x{f}", f"{kind}y{f}", f"{kind}t{f}")

    def borders(kind, f):
        arrived(f"{kind}u{f}", f"{kind}d{f}")

    def earlier(kind, f):
        arrived(f"{kind}t{f}", f"{kind}x{f}", f"{kind}y{f}")

    for ref, end in ((act, rows), (mid, half)):
        line = ref.shape[2:]

        @pl.when(t == 0)
        def _():
            ref[0:2] = jnp.zeros((2,) + ref.shape[1:], BF)

        for here, row in ((s == 0, 0), (s == ns - 1, end + 1)):
            @pl.when(here)
            def _():
                ref[2:, row] = jnp.zeros((frames,) + line, BF)

            @pl.when(jnp.logical_and(t > 0, here))
            def _():
                ref[0:2, row] = jnp.zeros((2,) + line, BF)

    @pl.when(s == 0)
    def _():
        fo[:, 0] = jnp.zeros((frames, pairs, 2 * c0), BF)

    for slot in (0, 1, 3):
        u1[slot, :, 0:c0, 2 * c0:3 * c0] = jnp.zeros((3, c0, c0), BF)
        u1[slot, :, c0:2 * c0, 3 * c0:4 * c0] = jnp.zeros((3, c0, c0), BF)
    wd[:, 0:c0, c1:2 * c1] = jnp.zeros((3, c0, c1), BF)

    step = 2

    def prepare(f, r, slot):
        count = step * cols
        base = slot * count
        lines[base:base + count] = raw[f, pl.ds(r, step)].reshape(count, c0).astype(F32)
        even = lines[pl.ds(base, count // 2, stride=2), :]
        odd = lines[pl.ds(base + 1, count // 2, stride=2), :]
        both = jnp.concatenate([even, odd], axis=1).reshape(step, pairs, 2 * c0)
        feat[f, pl.ds(r, step)] = both.astype(BF)
        act[f + 2, pl.ds(r + 1, step)] = silu(both).astype(BF)

    def own(f):
        def body(n, carry):
            for slot in range(4):
                prepare(f, (4 * n + slot) * step, slot)
            return carry

        lax.fori_loop(0, rows // (4 * step), body, 0)

    def taps(u, i):
        size = 32
        for r in range(0, u.shape[2], size):
            outer = u[0, i, r:r + size] + u[3, i, r:r + size]
            inner = u[1, i, r:r + size]
            u[1, i, r:r + size] = (outer + inner) * 0.5
            u[2, i, r:r + size] = (outer - inner) * 0.5

    def transform(src, dst, g):
        for n in range(dst.shape[2]):
            cells = products(*[src[g, 2 * n + j] for j in range(4)])
            for m in range(4):
                dst[g, m, n] = cells[m]

    def filtered(v, u, group, beside=None):
        width = v.shape[-1]
        size = v.shape[2] * pairs
        n_out = u.shape[-1]
        held = sums.at[:, 0:len(group) * size, 0:n_out]
        for m in range(4):
            left = jnp.concatenate(
                [
                    jnp.concatenate([v[f + i, m].reshape(size, width) for i in range(3)], axis=1)
                    for f in group
                ],
                axis=0,
            )
            right = u[m].reshape(3 * width, u.shape[-1])
            held[m] = jnp.dot(left, right, preferred_element_type=F32)
            if beside:
                beside(m)
        return held

    def combined(held, at, parity):
        part = pl.ds(at, pairs)
        one, two = held[1, part], held[2, part]
        return held[0, part] + one + two if parity == 0 else one - two - held[3, part]

    def conv_first(f, beside=None):
        bias = b1[...]
        held = filtered(v1, u1, [f], beside)
        for n in range(half):
            for parity in range(2):
                total = combined(held, n * pairs, parity)
                base = feat[f, 2 * n + parity].astype(F32)
                even = base[:, :c0] + bias + total[:, :c0] + before(total[:, 2 * c0:3 * c0], pairs)
                odd = base[:, c0:] + bias + total[:, c0:2 * c0] + after(total[:, 3 * c0:], pairs)
                fo[f, 2 * n + parity + 1] = jnp.concatenate([even, odd], axis=1).astype(BF)
        start(f"fo{f}")

    def downsample(f):
        arrived(f"fo{f}")
        left = jnp.concatenate(
            [
                jnp.concatenate([fo[f, 2 * r + j][None] for r in range(half)], axis=0).reshape(half * pairs, 2 * c0)
                for j in range(3)
            ],
            axis=1,
        )
        held = sums.at[0, 0:half * pairs, 0:2 * c1]
        held[...] = jnp.dot(left, wd[...].reshape(3 * 2 * c0, 2 * c1), preferred_element_type=F32)
        for n in range(half):
            total = held[n * pairs:(n + 1) * pairs]
            value = (total[:, :c1] + before(total[:, c1:], pairs) + bd[...]).astype(BF)
            red[f, n] = value
            mid[f + 2, n + 1] = silu(value.astype(F32)).astype(BF)
        send_borders("m", f)
        send_later("m", f)

    def conv_second(group):
        quarter = half // 2
        held = filtered(v2, u2, group)
        for g, f in enumerate(group):
            for n in range(quarter):
                for parity in range(2):
                    total = combined(held, (g * quarter + n) * pairs, parity)
                    value = red[f, 2 * n + parity].astype(F32) + b2[...] + total[:, c1:2 * c1]
                    value = value + before(total[:, :c1], pairs) + after(total[:, 2 * c1:], pairs)
                    res[f, 2 * n + parity] = value.astype(BF)
            pltpu.make_async_copy(res.at[f], out.at[f], osem.at[f]).start()

    inner = list(range(step, rows - step, step))

    def prepare_first(m):
        for n in inner[m::4]:
            prepare(0, n, m)

    def second_taps(m):
        if m < 3:
            taps(u2, m)

    for f in range(last, 0, -1):
        loads[f].wait()
        own(f)
        if f == last:
            pl.semaphore_wait(barrier, near_t * near_s - 1)
        send_borders("a", f)
    loads[0].wait()
    prepare(0, 0, 0)
    prepare(0, rows - step, 1)
    send_borders("a", 0)
    send_later("a", last)
    for copy in weights[:n_first]:
        copy.wait()
    for i in range(3):
        taps(u1, i)
    for f in range(last, 0, -1):
        borders("a", f)
        transform(act, v1, f + 2)
    conv_first(last, prepare_first)
    send_later("a", prev)
    for copy in weights[n_first:]:
        copy.wait()
    borders("a", 0)
    transform(act, v1, 2)
    conv_first(prev, second_taps)
    downsample(last)
    earlier("a", last)
    transform(act, v1, 1)
    conv_first(1)
    downsample(prev)
    earlier("a", prev)
    transform(act, v1, 0)
    conv_first(0)
    downsample(1)
    for f in (last, prev):
        borders("m", f)
        transform(mid, v2, f + 2)
    downsample(0)
    borders("m", 1)
    transform(mid, v2, 3)
    conv_second([last])
    borders("m", 0)
    for f in (last, prev):
        earlier("m", f)
    for g in range(3):
        transform(mid, v2, g)
    conv_second(list(range(prev, -1, -1)))

    for name in plan:
        @pl.when(there(*plan[name][3:]))
        def _():
            remote(name).wait_send()
    for f in range(frames):
        pltpu.make_async_copy(res.at[f], out.at[f], osem.at[f]).wait()


def on_device(nt, ns, x, k1, b1, kd, bd, k2, b2):
    frames, rows, cols, c0 = x.shape
    c1 = kd.shape[-1]
    half, pairs = rows // 2, cols // 2
    vmem = pl.BlockSpec(memory_space=pltpu.VMEM)
    hbm = pl.BlockSpec(memory_space=pl.ANY)
    copies = 5 * frames + 12
    return pl.pallas_call(
        functools.partial(kernel, nt, ns),
        out_shape=jax.ShapeDtypeStruct((frames, half, pairs, c1), BF),
        in_specs=[hbm] + [vmem] * 3 + [hbm] * 3,
        out_specs=hbm,
        scratch_shapes=[
            pltpu.VMEM((frames, rows, cols, c0), BF),
            pltpu.VMEM((8 * cols, c0), F32),
            pltpu.VMEM((frames + 2, rows + 2, pairs, 2 * c0), BF),
            pltpu.VMEM((frames, rows, pairs, 2 * c0), BF),
            pltpu.VMEM((frames + 2, 4, half, pairs, 2 * c0), BF),
            pltpu.VMEM((4, 3, 2 * c0, 4 * c0), BF),
            pltpu.VMEM((3, 2 * c0, 2 * c1), BF),
            pltpu.VMEM((frames + 2, 4, half // 2, pairs, c1), BF),
            pltpu.VMEM((4, 3, c1, 3 * c1), BF),
            pltpu.VMEM((frames, rows + 1, pairs, 2 * c0), BF),
            pltpu.VMEM((frames, half, pairs, c1), BF),
            pltpu.VMEM((frames + 2, half + 2, pairs, c1), BF),
            pltpu.VMEM((frames, half, pairs, c1), BF),
            pltpu.VMEM((4, max(half, 3 * half // 2) * pairs, 3 * c1), F32),
            pltpu.SemaphoreType.DMA((copies,)),
            pltpu.SemaphoreType.DMA((copies,)),
            pltpu.SemaphoreType.DMA((30,)),
            pltpu.SemaphoreType.DMA((frames,)),
            pltpu.SemaphoreType.DMA((frames,)),
        ],
        compiler_params=pltpu.CompilerParams(
            collective_id=0, has_side_effects=True, vmem_limit_bytes=60 * 1024 * 1024
        ),
        cost_estimate=pl.CostEstimate(flops=16 * 10**9, bytes_accessed=10**7, transcendentals=0),
    )(x, b1[None], bd[None], b2[None], k1, kd, k2)


def solution(mesh):
    in_specs = (P("tm", "space", None, None), P(), P(), P(), P(), P(), P())
    out_specs = P("tm", "space", None, None)
    sizes = mesh.shape["tm"], mesh.shape["space"]
    return jax.shard_map(
        functools.partial(on_device, *sizes), mesh=mesh, in_specs=in_specs, out_specs=out_specs, check_vma=False
    )
```

```python
import functools

import jax
import jax.numpy as jnp
from jax import lax
from jax.experimental import pallas as pl
from jax.experimental.pallas import tpu as pltpu
from jax.sharding import PartitionSpec as P

MESH = pl.DeviceIdType.MESH
BF = jnp.bfloat16
F32 = jnp.float32


def silu(v):
    h = 0.5 * v
    return h + h * jnp.tanh(h)


def edge(shape, width, row):
    at = lax.broadcasted_iota(jnp.int32, (width, shape[1]), 0) == row
    return jnp.broadcast_to(at[None], (shape[0] // width,) + at.shape).reshape(shape)


def before(x, width):
    return jnp.where(edge(x.shape, width, 0), 0.0, pltpu.roll(x, 1, 0))


def after(x, width):
    return jnp.where(edge(x.shape, width, width - 1), 0.0, pltpu.roll(x, x.shape[0] - 1, 0))


def products(d0, d1, d2, d3):
    return d0 - d2, d1 + d2, d2 - d1, d1 - d3


def kernel(
    nt, ns, x, b1, bd, b2, k1, kd, k2, out,
    raw, lines, act, feat, v1, u1, wd, v2, u2, fo, red, mid, res, sums,
    send, recv, wsem, osem, xsem,
):
    t, s = lax.axis_index("tm"), lax.axis_index("space")
    frames, rows, cols, c0 = x.shape
    pairs = cols // 2
    half = rows // 2
    c1 = res.shape[-1]

    def there(dt, ds):
        ok = None
        for pos, step, count in ((t, dt, nt), (s, ds, ns)):
            if step:
                this = pos < count - 1 if step > 0 else pos > 0
                ok = this if ok is None else jnp.logical_and(ok, this)
        return ok

    around = [(dt, ds) for dt in (-1, 0, 1) for ds in (-1, 0, 1) if dt or ds]

    def place(dt, ds):
        return (lax.rem(t + dt + nt, nt), lax.rem(s + ds + ns, ns))

    moves = []
    for j, slot in ((0, 0), (1, 1), (2, 3)):
        for k, blocks in ((0, ((0, 1), (1, 2))), (1, ((0, 0), (1, 1))), (2, ((0, 3), (1, 0)))):
            for a, b in blocks:
                moves.append((k1.at[:, j, k], u1.at[slot, :, a * c0:(a + 1) * c0, b * c0:(b + 1) * c0]))
    n_first = len(moves)
    moves.append((kd.at[:, 1], wd.at[:, 0:c0, 0:c1]))
    moves.append((kd.at[:, 2], wd.at[:, c0:2 * c0, 0:c1]))
    moves.append((kd.at[:, 0], wd.at[:, c0:2 * c0, c1:2 * c1]))
    n_down = len(moves)
    for j, slot in ((0, 0), (1, 1), (2, 3)):
        for k in range(3):
            moves.append((k2.at[:, j, k], u2.at[slot, :, :, k * c1:(k + 1) * c1]))
    loads = [pltpu.make_async_copy(x.at[f], raw.at[f], xsem.at[f]) for f in range(frames)]
    for copy in reversed(loads):
        copy.start()
    weights = [pltpu.make_async_copy(src, dst, wsem.at[n]) for n, (src, dst) in enumerate(moves)]
    for copy in weights:
        copy.start()

    barrier = pltpu.get_barrier_semaphore()
    for dt, ds in around:
        @pl.when(there(dt, ds))
        def _():
            pl.semaphore_signal(barrier, inc=1, device_id=place(dt, ds), device_id_type=MESH)
    near_t = jnp.where(t > 0, 1, 0) + jnp.where(t < nt - 1, 1, 0) + 1
    near_s = jnp.where(s > 0, 1, 0) + jnp.where(s < ns - 1, 1, 0) + 1

    plan = {}

    def add(name, src, dst, dt, ds):
        plan[name] = (src, dst, len(plan), dt, ds)

    last, prev = frames - 1, frames - 2
    for f in range(frames):
        add(f"fo{f}", fo.at[f, rows], fo.at[f, 0], 0, 1)
        for kind, ref, end in (("a", act, rows), ("m", mid, half)):
            add(f"{kind}u{f}", ref.at[f + 2, 1], ref.at[f + 2, end + 1], 0, -1)
            add(f"{kind}d{f}", ref.at[f + 2, end], ref.at[f + 2, 0], 0, 1)
            if f >= prev:
                g = f - prev
                add(f"{kind}t{f}", ref.at[f + 2, 1:end + 1], ref.at[g, 1:end + 1], 1, 0)
                add(f"{kind}x{f}", ref.at[f + 2, 1], ref.at[g, end + 1], 1, -1)
                add(f"{kind}y{f}", ref.at[f + 2, end], ref.at[g, 0], 1, 1)

    def remote(name):
        src, dst, n, dt, ds = plan[name]
        return pltpu.make_async_remote_copy(
            src_ref=src, dst_ref=dst, send_sem=send.at[n], recv_sem=recv.at[n],
            device_id=place(dt, ds), device_id_type=MESH,
        )

    def start(*names):
        for name in names:
            @pl.when(there(*plan[name][3:]))
            def _():
                remote(name).start()

    def arrived(*names):
        for name in names:
            _, _, _, dt, ds = plan[name]
            @pl.when(there(-dt, -ds))
            def _():
                remote(name).wait_recv()

    def send_borders(kind, f):
        start(f"{kind}u{f}", f"{kind}d{f}")

    def send_later(kind, f):
        if f >= prev:
            start(f"{kind}x{f}", f"{kind}y{f}", f"{kind}t{f}")

    def borders(kind, f):
        arrived(f"{kind}u{f}", f"{kind}d{f}")

    def earlier(kind, f):
        arrived(f"{kind}t{f}", f"{kind}x{f}", f"{kind}y{f}")

    for ref, end in ((act, rows), (mid, half)):
        line = ref.shape[2:]

        @pl.when(t == 0)
        def _():
            ref[0:2] = jnp.zeros((2,) + ref.shape[1:], BF)

        for here, row in ((s == 0, 0), (s == ns - 1, end + 1)):
            @pl.when(here)
            def _():
                ref[2:, row] = jnp.zeros((frames,) + line, BF)

            @pl.when(jnp.logical_and(t > 0, here))
            def _():
                ref[0:2, row] = jnp.zeros((2,) + line, BF)

    @pl.when(s == 0)
    def _():
        fo[:, 0] = jnp.zeros((frames, pairs, 2 * c0), BF)

    for slot in (0, 1, 3):
        u1[slot, :, 0:c0, 2 * c0:3 * c0] = jnp.zeros((3, c0, c0), BF)
        u1[slot, :, c0:2 * c0, 3 * c0:4 * c0] = jnp.zeros((3, c0, c0), BF)
    wd[:, 0:c0, c1:2 * c1] = jnp.zeros((3, c0, c1), BF)

    step = 2

    def prepare(f, r, slot):
        count = step * cols
        base = slot * count
        lines[base:base + count] = raw[f, pl.ds(r, step)].reshape(count, c0).astype(F32)
        even = lines[pl.ds(base, count // 2, stride=2), :]
        odd = lines[pl.ds(base + 1, count // 2, stride=2), :]
        both = jnp.concatenate([even, odd], axis=1).reshape(step, pairs, 2 * c0)
        feat[f, pl.ds(r, step)] = both.astype(BF)
        act[f + 2, pl.ds(r + 1, step)] = silu(both).astype(BF)

    def own(f):
        def body(n, carry):
            for slot in range(2):
                prepare(f, (2 * n + slot + 1) * step, slot)
            return carry

        lax.fori_loop(0, (rows // step - 2) // 2, body, 0)

    def taps(u, i):
        size = 32
        for r in range(0, u.shape[2], size):
            outer = u[0, i, r:r + size] + u[3, i, r:r + size]
            inner = u[1, i, r:r + size]
            u[1, i, r:r + size] = (outer + inner) * 0.5
            u[2, i, r:r + size] = (outer - inner) * 0.5

    def transform(src, dst, g):
        for n in range(dst.shape[2]):
            cells = products(*[src[g, 2 * n + j] for j in range(4)])
            for m in range(4):
                dst[g, m, n] = cells[m]

    def filtered(v, u, group, beside=None):
        width = v.shape[-1]
        size = v.shape[2] * pairs
        n_out = u.shape[-1]
        held = sums.at[:, 0:len(group) * size, 0:n_out]
        for m in range(4):
            left = jnp.concatenate(
                [
                    jnp.concatenate([v[f + i, m].reshape(size, width) for i in range(3)], axis=1)
                    for f in group
                ],
                axis=0,
            )
            right = u[m].reshape(3 * width, u.shape[-1])
            held[m] = jnp.dot(left, right, preferred_element_type=F32)
            if beside:
                beside(m)
        return held

    def combined(held, at, parity):
        part = pl.ds(at, pairs)
        one, two = held[1, part], held[2, part]
        return held[0, part] + one + two if parity == 0 else one - two - held[3, part]

    def conv_first(f, beside=None):
        bias = b1[...]
        held = filtered(v1, u1, [f], beside)
        for n in range(half):
            for parity in range(2):
                total = combined(held, n * pairs, parity)
                base = feat[f, 2 * n + parity].astype(F32)
                even = base[:, :c0] + bias + total[:, :c0] + before(total[:, 2 * c0:3 * c0], pairs)
                odd = base[:, c0:] + bias + total[:, c0:2 * c0] + after(total[:, 3 * c0:], pairs)
                fo[f, 2 * n + parity + 1] = jnp.concatenate([even, odd], axis=1).astype(BF)
        start(f"fo{f}")

    def downsample(f):
        arrived(f"fo{f}")
        left = jnp.concatenate(
            [
                jnp.concatenate([fo[f, 2 * r + j][None] for r in range(half)], axis=0).reshape(half * pairs, 2 * c0)
                for j in range(3)
            ],
            axis=1,
        )
        held = sums.at[0, 0:half * pairs, 0:2 * c1]
        held[...] = jnp.dot(left, wd[...].reshape(3 * 2 * c0, 2 * c1), preferred_element_type=F32)
        for n in range(half):
            total = held[n * pairs:(n + 1) * pairs]
            value = (total[:, :c1] + before(total[:, c1:], pairs) + bd[...]).astype(BF)
            red[f, n] = value
            mid[f + 2, n + 1] = silu(value.astype(F32)).astype(BF)
        send_borders("m", f)
        send_later("m", f)

    def conv_second(group):
        quarter = half // 2
        held = filtered(v2, u2, group)
        for g, f in enumerate(group):
            for n in range(quarter):
                for parity in range(2):
                    total = combined(held, (g * quarter + n) * pairs, parity)
                    value = red[f, 2 * n + parity].astype(F32) + b2[...] + total[:, c1:2 * c1]
                    value = value + before(total[:, :c1], pairs) + after(total[:, 2 * c1:], pairs)
                    res[f, 2 * n + parity] = value.astype(BF)
            pltpu.make_async_copy(res.at[f], out.at[f], osem.at[f]).start()

    inner = list(range(step, rows - step, step))

    def prepare_first(m):
        for n in inner[m::4]:
            prepare(0, n, m)

    def second_taps(m):
        if m < 3:
            taps(u2, m)

    for f in range(last, -1, -1):
        loads[f].wait()
        prepare(f, 0, 0)
        prepare(f, rows - step, 1)
        if f == last:
            pl.semaphore_wait(barrier, near_t * near_s - 1)
        send_borders("a", f)
    for f in range(last, 0, -1):
        own(f)
        if f == last:
            send_later("a", f)
    for copy in weights[:n_first]:
        copy.wait()
    for i in range(3):
        taps(u1, i)
    for f in range(last, 0, -1):
        borders("a", f)
        transform(act, v1, f + 2)
    conv_first(last, prepare_first)
    send_later("a", prev)
    for copy in weights[n_first:]:
        copy.wait()
    borders("a", 0)
    transform(act, v1, 2)
    conv_first(prev, second_taps)
    downsample(last)
    earlier("a", last)
    transform(act, v1, 1)
    conv_first(1)
    downsample(prev)
    earlier("a", prev)
    transform(act, v1, 0)
    conv_first(0)
    downsample(1)
    for f in (last, prev):
        borders("m", f)
        transform(mid, v2, f + 2)
    downsample(0)
    borders("m", 1)
    transform(mid, v2, 3)
    conv_second([last])
    borders("m", 0)
    transform(mid, v2, 2)
    conv_second([prev])
    for f in (last, prev):
        earlier("m", f)
        transform(mid, v2, f - prev)
    conv_second([1, 0])

    for name in plan:
        @pl.when(there(*plan[name][3:]))
        def _():
            remote(name).wait_send()
    for f in range(frames):
        pltpu.make_async_copy(res.at[f], out.at[f], osem.at[f]).wait()


def on_device(nt, ns, x, k1, b1, kd, bd, k2, b2):
    frames, rows, cols, c0 = x.shape
    c1 = kd.shape[-1]
    half, pairs = rows // 2, cols // 2
    vmem = pl.BlockSpec(memory_space=pltpu.VMEM)
    hbm = pl.BlockSpec(memory_space=pl.ANY)
    copies = 5 * frames + 12
    return pl.pallas_call(
        functools.partial(kernel, nt, ns),
        out_shape=jax.ShapeDtypeStruct((frames, half, pairs, c1), BF),
        in_specs=[hbm] + [vmem] * 3 + [hbm] * 3,
        out_specs=hbm,
        scratch_shapes=[
            pltpu.VMEM((frames, rows, cols, c0), BF),
            pltpu.VMEM((8 * cols, c0), F32),
            pltpu.VMEM((frames + 2, rows + 2, pairs, 2 * c0), BF),
            pltpu.VMEM((frames, rows, pairs, 2 * c0), BF),
            pltpu.VMEM((frames + 2, 4, half, pairs, 2 * c0), BF),
            pltpu.VMEM((4, 3, 2 * c0, 4 * c0), BF),
            pltpu.VMEM((3, 2 * c0, 2 * c1), BF),
            pltpu.VMEM((frames + 2, 4, half // 2, pairs, c1), BF),
            pltpu.VMEM((4, 3, c1, 3 * c1), BF),
            pltpu.VMEM((frames, rows + 1, pairs, 2 * c0), BF),
            pltpu.VMEM((frames, half, pairs, c1), BF),
            pltpu.VMEM((frames + 2, half + 2, pairs, c1), BF),
            pltpu.VMEM((frames, half, pairs, c1), BF),
            pltpu.VMEM((4, max(half, 3 * half // 2) * pairs, 3 * c1), F32),
            pltpu.SemaphoreType.DMA((copies,)),
            pltpu.SemaphoreType.DMA((copies,)),
            pltpu.SemaphoreType.DMA((30,)),
            pltpu.SemaphoreType.DMA((frames,)),
            pltpu.SemaphoreType.DMA((frames,)),
        ],
        compiler_params=pltpu.CompilerParams(
            collective_id=0, has_side_effects=True, vmem_limit_bytes=60 * 1024 * 1024
        ),
        cost_estimate=pl.CostEstimate(flops=16 * 10**9, bytes_accessed=10**7, transcendentals=0),
    )(x, b1[None], bd[None], b2[None], k1, kd, k2)


def solution(mesh):
    in_specs = (P("tm", "space", None, None), P(), P(), P(), P(), P(), P())
    out_specs = P("tm", "space", None, None)
    sizes = mesh.shape["tm"], mesh.shape["space"]
    return jax.shard_map(
        functools.partial(on_device, *sizes), mesh=mesh, in_specs=in_specs, out_specs=out_specs, check_vma=False
    )
```
